256 devices in a mesh: pipe: 4 (over z_hi, core), expert: 16 (over x, y), dp: 4 (over z_lo).
Axes of the slice: x: 4, y: 4, z: 8 (z_hi: 2, z_lo: 4; z = z_hi * 4 + z_lo), core: 2. Of those that a mesh axis runs over, the one named last changes fastest.
Arguments:
- cotangent: bfloat16 [4, 4, 2048, 3584], P('pipe', 'dp', 'expert'), may hold values from -0.125 to 0.125
- gates: float32 [4, 4, 2048, 8], P('pipe', 'dp', 'expert'), may hold values from 0.1 to 1
- routes: int32 [4, 4, 2048, 8], P('pipe', 'dp', 'expert'), may hold values from 0 to 15, all different within a row; in each aligned block of 128 rows (0 to 127, 128 to 255, ..., all dimensions but the last counted through in order) at most 80 rows name the same one
- saved_hidden: bfloat16 [4, 4, 16, 1280, 1024], P('pipe', 'dp', 'expert'), may hold values from -6 to 6
- master: float32 [4, 16, 512, 3584], P('pipe', 'expert', 'dp'), may hold values from -6 to 6
- first_moment: bfloat16 [4, 16, 512, 3584], P('pipe', 'expert', 'dp'), may hold values from -0.625 to 0.625
- second_moment: bfloat16 [4, 16, 512, 3584], P('pipe', 'expert', 'dp'), may hold values from 0.0099487305 to 1
- average: bfloat16 [4, 16, 512, 3584], P('pipe', 'expert', 'dp'), may hold values from -6 to 6
Outputs:
- master_new: float32 [4, 16, 512, 3584], P('pipe', 'expert', 'dp')
- first_new: bfloat16 [4, 16, 512, 3584], P('pipe', 'expert', 'dp')
- second_new: bfloat16 [4, 16, 512, 3584], P('pipe', 'expert', 'dp')
- average_new: bfloat16 [4, 16, 512, 3584], P('pipe', 'expert', 'dp')
The draws below stay inside these ranges and needn't reach their ends.
Inputs may be any that keep to these rules, and one draw needn't show every extreme that they name: `routes`: each token names 8 distinct experts. Among the tokens of one device, at most 80 name any one expert; on some devices one expert is named by exactly 80 of them.
All inputs are finite; a program needn't handle non-finite values.
Results may differ from the reference program's by a relative error of at most 0.015.
Values may be sent and summed in bfloat16 or wider, within the bound.
No kernel may reach another device: no remote copies, remote signals or barrier semaphores. Data moves between devices by JAX's collectives and lax.ppermute only.
A program may use at most 128 MiB of HBM per device.

```python
import math
import jax
import jax.numpy as jnp
import numpy as np
from jax import lax

D = 3584
FF = 1024
TOK_DEV = 128
EXPERTS = 16
TOP = 8
CAP = 80
TOKENS = 2048
SLOTS = 1280
N_PIPE = 4
N_EXPERT = 16
N_DP = 4


def shard_levels(rng, dims, shards, low, top_value):
    level = 1.0
    for axis_at, shards_of in shards:
        draws = jax.random.uniform(jax.random.fold_in(jax.random.fold_in(rng, 6), axis_at), (shards_of,), jnp.float32, low / len(shards), top_value / len(shards))
        level = level * jnp.repeat(jnp.exp(draws), dims[axis_at] // shards_of).reshape((-1,) + (1,) * (len(dims) - 1 - axis_at))
    return level


def assign_block(own_key, own, number, rows, amount, top, reach, slope):
    sequence = jax.random.permutation(own_key, amount)
    crowded, common = portions_of(amount, rows * top, reach, slope, True), portions_of(amount, rows * top, reach, slope, False)
    places = jnp.arange(amount)

    def named(sizes, turn):
        used = int((sizes > 0).sum())
        fixed = max(1, used // 4)
        moved = fixed + (places - fixed + turn * (used - fixed)) % max(1, amount - fixed)
        return jnp.zeros((amount,), jnp.int32).at[sequence[jnp.where(places < fixed, places, moved)]].set(jnp.asarray(sizes, jnp.int32))

    sizes = jnp.where(number % 4 == 0, named(crowded, number // 4), named(common, number - number // 4 - 1))
    mixed = jax.random.permutation(jax.random.fold_in(own, 3), amount)
    source_of, sink = mixed[0:amount // 2 * 2:2], mixed[1:amount // 2 * 2:2]
    margin = jnp.minimum(sizes[source_of] - 1, reach - sizes[sink]) // 2
    margin = jnp.where((source_of == sequence[0]) | (sink == sequence[0]) | (sizes[sink] == 0), 0, jnp.maximum(margin, 0))
    moved = jax.random.randint(jax.random.fold_in(own, 4), (amount // 2,), 0, 1 << 20) % (margin + 1)
    sizes = sizes.at[source_of].add(-moved).at[sink].add(moved)
    members = jnp.searchsorted(jnp.cumsum(sizes), jnp.arange(rows * top), side="right").astype(jnp.int32)
    listing = members.reshape(top, rows).T
    listing = listing[jax.random.permutation(jax.random.fold_in(own, 1), rows)]
    turn = jax.random.randint(jax.random.fold_in(own, 2), (rows, 1), 0, top)
    return jnp.take_along_axis(listing, (jnp.arange(top)[None, :] + turn) % top, axis=1)


def portions_of(count, total, bound, slope, full):
    weights = [(1 << 20) // math.isqrt(grade ** slope) + 1 for grade in range(1, count + 1)]
    largest = bound if full else min(bound, max(-(-total // count), total * weights[0] // sum(weights)))
    least = 1 if total - largest >= count - 1 else 0
    counts, rest = [largest] + [least] * (count - 1), total - largest - least * (count - 1)
    while rest > 0:
        free = [i for i in range(1, count) if counts[i] < largest] or [i for i in range(1, count) if counts[i] < bound]
        whole, budget = sum([weights[i] for i in free]), rest
        for i in free:
            more = min(bound - counts[i], max(1, budget * weights[i] // whole), rest)
            counts[i] = counts[i] + more
            rest = rest - more
    return np.array(counts)


def gaussian(key, shape, deviation, most, split=(), held_as=jnp.bfloat16):
    drawn = deviation * jax.random.normal(key, shape, jnp.float32)
    if split:
        drawn = drawn * shard_levels(key, shape, split, -0.22, 0.18)
    return jnp.clip(drawn, -most, most).astype(held_as)


def setup_inputs(seed: int = 0) -> dict:
    arg_keys = jax.random.split(jax.random.key(seed), 9)
    cotangent = gaussian(arg_keys[0], (N_PIPE, N_DP, TOKENS, D), 0.02, 0.125, ((0, 4), (1, 4), (2, 16)))
    gates = jnp.clip(0.1 + 0.9 * jax.random.uniform(arg_keys[1], (N_PIPE, N_DP, TOKENS, TOP), jnp.float32) ** shard_levels(arg_keys[1], (N_PIPE, N_DP, TOKENS, TOP), ((0, 4), (1, 4), (2, 16)), -0.2, 0.2), 0.1, 1.0)
    routes_keys = jax.random.split(jax.random.fold_in(arg_keys[2], 1), N_PIPE * N_DP * TOKENS // TOK_DEV)
    routes_turns = jax.random.permutation(jax.random.fold_in(arg_keys[2], 3), N_PIPE * N_DP * TOKENS // TOK_DEV)
    routes = jax.vmap(lambda own, number: assign_block(jax.random.fold_in(arg_keys[2], 2), own, number, TOK_DEV, EXPERTS, TOP, CAP, 2))(routes_keys, routes_turns).reshape((N_PIPE, N_DP, TOKENS, TOP))
    saved_hidden = gaussian(arg_keys[3], (N_PIPE, N_DP, EXPERTS, SLOTS, FF), 1.0, 6.0, ((0, 4), (1, 4), (2, 16)))
    master = gaussian(arg_keys[4], (N_PIPE, EXPERTS, FF // 2, D), 1.0, 6.0, ((0, 4), (1, 16), (2, 4)), jnp.float32)
    first_moment = gaussian(arg_keys[5], (N_PIPE, EXPERTS, FF // 2, D), 0.1, 0.625, ((0, 4), (1, 16), (2, 4)))
    second_moment = jnp.clip(jnp.exp(math.log(1.0) - 4.61031033 * jax.random.uniform(arg_keys[6], (N_PIPE, EXPERTS, FF // 2, D), jnp.float32) ** shard_levels(arg_keys[6], (N_PIPE, EXPERTS, FF // 2, D), ((0, 4), (1, 16), (2, 4)), -0.2, 0.2)), 0.0099487305, 1.0).astype(jnp.bfloat16)
    average = gaussian(arg_keys[7], (N_PIPE, EXPERTS, FF // 2, D), 1.0, 6.0, ((0, 4), (1, 16), (2, 4)))
    return {"cotangent": cotangent, "gates": gates, "routes": routes, "saved_hidden": saved_hidden, "master": master, "first_moment": first_moment, "second_moment": second_moment, "average": average}


beta_one = 0.9
beta_two = 0.95
epsilon = 1e-08
learn_rate = 0.00022
weight_decay = 0.1
average_decay = 0.999

def section_terms(cotangent, gates, routes, saved_hidden, section, replica, expert):
    route = routes[section, replica]
    matched = route == expert
    member = jnp.any(matched, axis=1)
    weight = lax.optimization_barrier(jnp.sum(jnp.where(matched, gates[section, replica], 0.0), axis=1))
    grouped = member.astype(jnp.int32).reshape(N_EXPERT, TOK_DEV)
    position = jnp.cumsum(grouped, axis=1) - 1
    source = jnp.arange(N_EXPERT, dtype=jnp.int32)[:, None]
    slot = (source * CAP + position).reshape(TOKENS)
    clamped = jnp.where(member, slot, 0).astype(jnp.int32)
    hidden = lax.dynamic_index_in_dim(saved_hidden[section, replica], expert, 0, keepdims=False)
    picked = jnp.take(hidden, clamped, axis=0)
    scaled = (weight[:, None] * cotangent[section, replica].astype(jnp.float32)).astype(jnp.bfloat16)
    return (picked, scaled)

def pair_gradient(cotangent, gates, routes, saved_hidden, sections):

    def one_expert(expert):
        pieces = [section_terms(cotangent, gates, routes, saved_hidden, section, replica, expert) for section in sections for replica in range(N_DP)]
        hidden_rows = jnp.concatenate([piece[0] for piece in pieces], axis=0)
        slot_rows = jnp.concatenate([piece[1] for piece in pieces], axis=0)
        return lax.dot_general(hidden_rows, slot_rows, (((0,), (0,)), ((), ())), preferred_element_type=jnp.float32)
    return lax.map(one_expert, jnp.arange(EXPERTS, dtype=jnp.int32))

def reference(cotangent, gates, routes, saved_hidden, master, first_moment, second_moment, average):
    eighth = FF // (2 * N_DP)
    blocks = [None] * N_PIPE
    for front_section in range(N_PIPE // 2):
        mirror_section = N_PIPE - 1 - front_section
        summed = pair_gradient(cotangent, gates, routes, saved_hidden, (front_section, mirror_section))
        summed = summed.reshape(EXPERTS, N_DP, 2, eighth, D)
        blocks[front_section] = summed[:, :, 0].reshape(EXPERTS, FF // 2, D)
        blocks[mirror_section] = summed[:, :, 1].reshape(EXPERTS, FF // 2, D)
    gradient = jnp.stack(blocks)
    moment_one = beta_one * first_moment.astype(jnp.float32) + (1.0 - beta_one) * gradient
    moment_two = beta_two * second_moment.astype(jnp.float32) + (1.0 - beta_two) * gradient * gradient
    master_new = master - learn_rate * (moment_one / (jnp.sqrt(moment_two) + epsilon) + weight_decay * master)
    average_new = average_decay * average.astype(jnp.float32) + (1.0 - average_decay) * master_new
    return (master_new, moment_one.astype(jnp.bfloat16), moment_two.astype(jnp.bfloat16), average_new.astype(jnp.bfloat16))
```

```python
import jax
import jax.numpy as jnp
from jax import lax
from jax.sharding import PartitionSpec as P

beta_one = 0.9
beta_two = 0.95
epsilon = 1e-08
learn_rate = 0.00022
weight_decay = 0.1
average_decay = 0.999

SIDE = 4
RING = 8
PARTS = ((0, 1792), (1792, 1792))
GATHERS = 2


def torus_pairs(axis):
    pairs = []
    for section in range(4):
        way = 1 if section % 2 == 0 else -1
        for x in range(SIDE):
            for y in range(SIDE):
                to_x, to_y = ((x + way) % SIDE, y) if axis == 0 else (x, (y + way) % SIDE)
                pairs.append((section * 16 + x * SIDE + y, section * 16 + to_x * SIDE + to_y))
    return pairs


def torus_step(value, axis):
    return lax.ppermute(value, ("pipe", "expert"), torus_pairs(axis))


def ring_place(z, kind):
    high, low = z // 4, z % 4
    return (high * 2 + (kind ^ high)) * 4 + low


RING_GROUPS = [[ring_place(z, kind) for z in range(RING)] for kind in range(2)]


def first_phase(rows, axis):
    pieces = [rows]
    for _ in range(SIDE - 1):
        pieces.append(torus_step(pieces[-1], axis))
    return pieces


def token_rows(hidden, slot, weight, order):
    blocks = jnp.take(hidden, order, axis=0)
    slot = jnp.take(slot, order, axis=0)
    weight = jnp.take(weight, order, axis=0)
    onehot = (slot[:, :, None] == jnp.arange(hidden.shape[1], dtype=jnp.float32)).astype(jnp.bfloat16)
    picked = jnp.einsum("stc,scf->stf", onehot, blocks, preferred_element_type=jnp.float32)
    return (picked * weight[:, :, None]).astype(jnp.bfloat16)


def contract(rows, cotangent):
    return lax.dot_general(rows, cotangent, (((0,), (0,)), ((), ())), preferred_element_type=jnp.float32)


def update(gradient, master, first_moment, second_moment, average):
    moment_one = beta_one * first_moment.astype(jnp.float32) + (1.0 - beta_one) * gradient
    moment_two = beta_two * second_moment.astype(jnp.float32) + (1.0 - beta_two) * gradient * gradient
    master_new = master - learn_rate * (
        moment_one / (jnp.sqrt(moment_two) + epsilon) + weight_decay * master
    )
    average_new = average_decay * average.astype(jnp.float32) + (1.0 - average_decay) * master_new
    return (
        master_new,
        moment_one.astype(jnp.bfloat16),
        moment_two.astype(jnp.bfloat16),
        average_new.astype(jnp.bfloat16),
    )


def shards(cotangent, gates, routes, saved_hidden, master, first_moment, second_moment, average):
    tokens_here = cotangent[0, 0]
    route = routes[0, 0]
    gate = gates[0, 0]
    hidden = saved_hidden[0, 0, 0]
    expert_count = lax.axis_size("expert")
    capacity = hidden.shape[0] // expert_count
    half = tokens_here.shape[0] // 2
    inner = hidden.shape[1]
    me = lax.axis_index("expert")
    section = lax.axis_index("pipe")

    matches = route[:, :, None] == jnp.arange(expert_count, dtype=jnp.int32)[None, None, :]
    member = jnp.any(matches, axis=1)
    weight = jnp.sum(jnp.where(matches, gate[:, :, None], 0.0), axis=1)
    position = jnp.cumsum(member.astype(jnp.int32), axis=0) - 1
    slot = jnp.where(member, position, -1).astype(jnp.float32)
    table = jnp.stack([slot.T, weight.T], axis=1)
    tables = lax.all_gather(table, "expert")
    mine = lax.dynamic_index_in_dim(tables, me, 1, keepdims=False)
    slot, weight = mine[:, 0], mine[:, 1]

    way = 1 - 2 * (section % 2)
    steps = jnp.arange(SIDE, dtype=jnp.int32)
    at_x, at_y = me // SIDE, me % SIDE
    along_x = (at_x - way * steps) % SIDE
    along_y = (at_y - way * steps) % SIDE
    order_a = (along_x[None, :] * SIDE + along_y[:, None]).reshape(-1)
    order_b = (along_x[:, None] * SIDE + along_y[None, :]).reshape(-1)
    blocks = hidden.reshape(expert_count, capacity, 4, 2, inner // RING)
    blocks = blocks.transpose(0, 1, 3, 2, 4).reshape(expert_count, capacity, inner)
    rows_a = token_rows(blocks, slot[:, :half], weight[:, :half], order_a)
    rows_b = token_rows(blocks, slot[:, half:], weight[:, half:], order_b)
    rows_a = rows_a.reshape(SIDE, SIDE * half, inner)
    rows_b = rows_b.reshape(SIDE, SIDE * half, inner)

    phase_one = []
    for start, width in PARTS:
        part = tokens_here[:, start : start + width]
        phase_one.append((first_phase(part[:half], 0), first_phase(part[half:], 1)))
    gradients = []
    for (start, width), (pieces_a, pieces_b) in zip(PARTS, phase_one):
        piece = width // GATHERS
        sums = []
        for g in range(GATHERS):
            at = g * piece
            a = jnp.concatenate([p[:, at : at + piece] for p in pieces_a], 0)
            b = jnp.concatenate([p[:, at : at + piece] for p in pieces_b], 0)
            total = contract(rows_a[0], a) + contract(rows_b[0], b)
            for step in range(1, SIDE):
                a = torus_step(a, 1)
                b = torus_step(b, 0)
                total = total + contract(rows_a[step], a) + contract(rows_b[step], b)
            sums.append(total.astype(jnp.bfloat16))
        gradients.append(
            lax.psum_scatter(
                jnp.concatenate(sums, 1),
                ("pipe", "dp"),
                scatter_dimension=0,
                axis_index_groups=RING_GROUPS,
                tiled=True,
            )
        )
    gradient = jnp.concatenate(gradients, 1).astype(jnp.float32).reshape(master.shape)
    return update(gradient, master, first_moment, second_moment, average)


def solution(mesh):
    rows = P("pipe", "dp", "expert", None)
    states = P("pipe", "expert", "dp", None)
    return jax.shard_map(
        shards,
        mesh=mesh,
        in_specs=(rows, rows, rows, P("pipe", "dp", "expert", None, None)) + (states,) * 4,
        out_specs=(states,) * 4,
        check_vma=False,
    )
```

```python
import functools

import jax
import jax.numpy as jnp
from jax import lax
from jax.experimental import pallas as pl
from jax.experimental.pallas import tpu as pltpu
from jax.sharding import PartitionSpec as P

beta_one = 0.9
beta_two = 0.95
epsilon = 1e-08
learn_rate = 0.00022
weight_decay = 0.1
average_decay = 0.999

SIDE = 4
RING = 8
QUARTERS = 4
GROUPS = ((0, 1792), (1792, 1792))
SUMS = ("ring", "tree")
TILE = 256
LANES = 128


def torus_pairs(axis):
    pairs = []
    for section in range(4):
        way = 1 if section % 2 == 0 else -1
        for x in range(SIDE):
            for y in range(SIDE):
                to_x, to_y = ((x + way) % SIDE, y) if axis == 0 else (x, (y + way) % SIDE)
                pairs.append((section * 16 + x * SIDE + y, section * 16 + to_x * SIDE + to_y))
    return pairs


def torus_step(value, axis):
    return lax.ppermute(value, ("pipe", "expert"), torus_pairs(axis))


def ring_place(z, kind):
    high, low = z // 4, z % 4
    return (high * 2 + (kind ^ high)) * 4 + low


def ring_step(value, ways):
    pairs = [(ring_place(z, kind), ring_place((z + ways[kind]) % RING, kind)) for kind in range(2) for z in range(RING)]
    return lax.ppermute(value, ("pipe", "dp"), pairs)


def first_kernel(route_ref, gate_ref, cotangent_ref, *out_refs):
    tokens, width = cotangent_ref.shape
    shape = (tokens, LANES)
    lane = lax.broadcasted_iota(jnp.int32, shape, 1)
    expert = lane >> 2
    member = jnp.zeros(shape, jnp.float32)
    weight = jnp.zeros(shape, jnp.float32)
    for k in range(route_ref.shape[1]):
        match = route_ref[:, k : k + 1] == expert
        member = member + jnp.where(match, 1.0, 0.0)
        weight = weight + jnp.where(match, gate_ref[:, k : k + 1], 0.0)
    before = lax.broadcasted_iota(jnp.int32, (tokens, tokens), 1) < lax.broadcasted_iota(jnp.int32, (tokens, tokens), 0)
    position = jnp.dot(
        before.astype(jnp.float32).astype(jnp.bfloat16),
        member.astype(jnp.bfloat16),
        preferred_element_type=jnp.float32,
    )
    high = weight.astype(jnp.bfloat16).astype(jnp.float32)
    middle = (weight - high).astype(jnp.bfloat16).astype(jnp.float32)
    low = weight - high - middle
    kind = lane & 3
    table = jnp.where(member > 0.5, position, -1.0)
    table = jnp.where(kind == 0, table, jnp.where(kind == 1, high, jnp.where(kind == 2, middle, low)))
    table = table.astype(jnp.bfloat16)
    quarter = tokens // QUARTERS
    for q, out_ref in enumerate(out_refs):
        out_ref[:, :width] = cotangent_ref[q * quarter : (q + 1) * quarter, :]
        out_ref[:, width:] = table[q * quarter : (q + 1) * quarter, :]


def first_lines(route, gate, cotangent):
    tokens, width = cotangent.shape
    return pl.pallas_call(
        first_kernel,
        out_shape=[jax.ShapeDtypeStruct((tokens // QUARTERS, width + LANES), jnp.bfloat16)] * QUARTERS,
        compiler_params=pltpu.CompilerParams(vmem_limit_bytes=16 * 1024 * 1024),
        name="first_lines",
    )(route, gate, cotangent)


def rows_kernel(order_ref, *refs):
    hidden_refs, table_refs, out_ref, table_scr = refs[:SIDE], refs[SIDE : SIDE + QUARTERS], refs[-2], refs[-1]
    for q in range(QUARTERS):

        @pl.when(pl.program_id(0) == q)
        def _():
            table_scr[...] = table_refs[q][...].astype(jnp.float32)

    table = table_scr[...]
    lane = lax.broadcasted_iota(jnp.int32, table.shape, 1) - 4 * order_ref[QUARTERS * SIDE]
    slot = jnp.sum(jnp.where(lane == 0, table, 0.0), axis=1, keepdims=True).astype(jnp.int32)
    weight = jnp.sum(jnp.where((lane > 0) & (lane < 4), table, 0.0), axis=1, keepdims=True)
    tokens = table.shape[0] // SIDE
    parts = []
    for s, hidden_ref in enumerate(hidden_refs):
        capacity = hidden_ref.shape[1]
        here = slice(s * tokens, (s + 1) * tokens)
        chosen = lax.broadcasted_iota(jnp.int32, (tokens, capacity), 1) == slot[here]
        picked = jnp.dot(
            chosen.astype(jnp.float32).astype(jnp.bfloat16), hidden_ref[0], preferred_element_type=jnp.float32
        )
        parts.append(picked * weight[here])
    rows = jnp.concatenate(parts, axis=0).T.astype(jnp.bfloat16)
    unit = rows.shape[0] // RING
    for z in range(RING):
        at = (z % 4) * 2 + z // 4
        out_ref[z * unit : (z + 1) * unit, :] = rows[at * unit : (at + 1) * unit, :]


def token_rows(hidden, order, lines):
    sources, capacity, inner = hidden.shape
    height, width = lines[0].shape

    def hidden_spec(s):
        return pl.BlockSpec((1, capacity, inner), lambda i, order_ref, s=s: (order_ref[i * SIDE + s], 0, 0))

    return pl.pallas_call(
        rows_kernel,
        out_shape=jax.ShapeDtypeStruct((inner, QUARTERS * height), jnp.bfloat16),
        grid_spec=pltpu.PrefetchScalarGridSpec(
            num_scalar_prefetch=1,
            grid=(QUARTERS,),
            in_specs=[hidden_spec(s) for s in range(SIDE)]
            + [pl.BlockSpec((height, LANES), lambda i, order_ref: (0, width // LANES - 1))] * QUARTERS,
            out_specs=pl.BlockSpec((inner, height), lambda i, order_ref: (0, i)),
            scratch_shapes=[pltpu.VMEM((height, LANES), jnp.float32)],
        ),
        compiler_params=pltpu.CompilerParams(vmem_limit_bytes=16 * 1024 * 1024),
        cost_estimate=pl.CostEstimate(flops=10**9, bytes_accessed=4 * 10**6, transcendentals=0),
        name="token_rows",
    )(order, *([hidden] * SIDE), *lines)


def assemble_kernel(spans, *refs):
    pieces, outs, sems = refs[: QUARTERS * SIDE], refs[-QUARTERS - 1 : -1], refs[-1]
    tokens = pieces[0].shape[0]
    copies = []
    for q in range(QUARTERS):
        for s in range(SIDE):
            to = 0
            for start, width in spans:
                copies.append(
                    pltpu.make_async_copy(
                        pieces[q * SIDE + s].at[:, start : start + width],
                        outs[q].at[s * tokens : (s + 1) * tokens, to : to + width],
                        sems.at[len(copies)],
                    )
                )
                to += width
    for copy in copies:
        copy.start()
    for copy in copies:
        copy.wait()


def assemble(first, spans, before):
    tokens = first[0][0].shape[0]
    width = sum(w for _, w in spans)
    anywhere = pl.BlockSpec(memory_space=pl.ANY)
    return pl.pallas_call(
        functools.partial(assemble_kernel, spans),
        out_shape=[jax.ShapeDtypeStruct((SIDE * tokens, width), jnp.bfloat16)] * QUARTERS,
        in_specs=[anywhere] * (QUARTERS * SIDE + len(before)),
        out_specs=[anywhere] * QUARTERS,
        scratch_shapes=[pltpu.SemaphoreType.DMA((QUARTERS * SIDE * len(spans),))],
        compiler_params=pltpu.CompilerParams(vmem_limit_bytes=1024 * 1024),
        cost_estimate=pl.CostEstimate(flops=0, bytes_accessed=4 * QUARTERS * SIDE * tokens * width, transcendentals=0),
        name="assemble",
    )(*[piece for pieces in first for piece in pieces], *before)


def contract_kernel(steps, more, *refs):
    rows_refs, pieces, out_ref = refs[:steps], refs[steps : steps * (1 + QUARTERS)], refs[-1]
    total = refs[steps * (1 + QUARTERS)][...] if more else None
    for step, rows_ref in enumerate(rows_refs):
        here = pieces[step * QUARTERS : (step + 1) * QUARTERS]
        cotangent = jnp.concatenate([piece[...] for piece in here], axis=0)
        part = jnp.dot(rows_ref[...], cotangent, preferred_element_type=jnp.float32)
        total = part if total is None else total + part
    out_ref[...] = total.astype(out_ref.dtype)


def contract(rows, lines, width, dtype, more=()):
    inner, depth = rows[0].shape
    pieces = [piece for step in lines for piece in step]
    height = pieces[0].shape[0]
    return pl.pallas_call(
        functools.partial(contract_kernel, len(rows), len(more)),
        out_shape=jax.ShapeDtypeStruct((inner, width), dtype),
        grid=(width // TILE,),
        in_specs=[pl.BlockSpec((inner, depth), lambda i: (0, 0), pipeline_mode=pl.Buffered(1))] * len(rows)
        + [pl.BlockSpec((height, TILE), lambda i: (0, i))] * len(pieces)
        + [pl.BlockSpec((inner, TILE), lambda i: (0, i))] * len(more),
        out_specs=pl.BlockSpec((inner, TILE), lambda i: (0, i)),
        compiler_params=pltpu.CompilerParams(vmem_limit_bytes=16 * 1024 * 1024),
        cost_estimate=pl.CostEstimate(
            flops=2 * inner * depth * len(rows) * width,
            bytes_accessed=6 * inner * width,
            transcendentals=0,
        ),
        name="contract",
    )(*rows, *pieces, *more)


def ring_sum(terms, height, way):
    def term(owner):
        return lax.dynamic_index_in_dim(terms, owner % RING, 0, keepdims=False).astype(jnp.float32)

    total = term(height - way)
    for step in range(2, RING + 1):
        total = ring_step(total.astype(jnp.bfloat16), (1, -1)).astype(jnp.float32) + term(height - way * step)
    return total


def tree_sum(terms, height):
    def term(distance):
        return lax.dynamic_index_in_dim(terms, (height + distance) % RING, 0, keepdims=False).astype(jnp.float32)

    def send(value, way):
        return ring_step(value.astype(jnp.bfloat16), (way, way)).astype(jnp.float32)

    far = term(RING // 2)
    middle = far.shape[0] // 2
    up, down = send(far[:middle], 1), send(far[middle:], -1)
    near_up, near_down = term(3), term(5)
    up = jnp.concatenate([near_up[:middle] + up, near_up[middle:]], 0)
    down = jnp.concatenate([near_down[:middle], near_down[middle:] + down], 0)
    up, down = send(up, 1), send(down, -1)
    up, down = send(up + term(2), 1), send(down + term(6), -1)
    up, down = send(up + term(1), 1), send(down + term(7), -1)
    return term(0) + up + down


def update(gradient, master, first_moment, second_moment, average):
    moment_one = beta_one * first_moment.astype(jnp.float32) + (1.0 - beta_one) * gradient
    moment_two = beta_two * second_moment.astype(jnp.float32) + (1.0 - beta_two) * gradient * gradient
    master_new = master - learn_rate * (
        moment_one / (jnp.sqrt(moment_two) + epsilon) + weight_decay * master
    )
    average_new = average_decay * average.astype(jnp.float32) + (1.0 - average_decay) * master_new
    return (
        master_new,
        moment_one.astype(jnp.bfloat16),
        moment_two.astype(jnp.bfloat16),
        average_new.astype(jnp.bfloat16),
    )


def shards(cotangent, gates, routes, saved_hidden, master, first_moment, second_moment, average):
    tokens_here = cotangent[0, 0]
    route = routes[0, 0]
    gate = gates[0, 0]
    hidden = saved_hidden[0, 0, 0]
    expert_count = lax.axis_size("expert")
    capacity = hidden.shape[0] // expert_count
    quarter = tokens_here.shape[0] // QUARTERS
    inner = hidden.shape[1]
    me = lax.axis_index("expert")
    section = lax.axis_index("pipe")
    height = (section // 2) * 4 + lax.axis_index("dp")

    first = [[piece] for piece in first_lines(route, gate, tokens_here)]
    for _ in range(SIDE - 1):
        for q in range(QUARTERS):
            first[q].append(torus_step(first[q][-1], 0 if q < 2 else 1))

    way = 1 - 2 * (section % 2)
    steps = jnp.arange(SIDE, dtype=jnp.int32)
    at_x, at_y = me // SIDE, me % SIDE
    along_x = (at_x - way * steps) % SIDE
    along_y = (at_y - way * steps) % SIDE
    order_a = along_x[None, :] * SIDE + along_y[:, None]
    order_b = along_x[:, None] * SIDE + along_y[None, :]
    hidden = hidden.reshape(expert_count, capacity, inner)

    rows, sums, last = [], [], None
    for g, (start, width) in enumerate(GROUPS):
        spans = ((start, width),) if g else ((start, width), (tokens_here.shape[1], LANES))
        lines = [assemble(first, spans, last[2] if g else [])]
        for _ in range(SIDE - 1):
            lines.append([torus_step(lines[-1][q], 1 if q < 2 else 0) for q in range(QUARTERS)])
        if not g:
            for step in range(SIDE):
                order = jnp.concatenate([order_a[step], order_a[step], order_b[step], order_b[step], me[None]])
                rows.append(token_rows(hidden, order, lines[step]))
        part = contract(rows[:-1], lines[:-1], width, jnp.float32)
        sums.append(contract(rows[-1:], lines[-1:], width, jnp.bfloat16, [part]))
        last = lines

    gradients = []
    for kind, terms in zip(SUMS, sums):
        terms = terms.reshape(RING, -1, terms.shape[1])
        if kind == "ring":
            gradients.append(ring_sum(terms, height, 1 - 2 * (section % 2 ^ section // 2)))
        else:
            gradients.append(tree_sum(terms, height))
    gradient = jnp.concatenate(gradients, 1).reshape(master.shape)
    return update(gradient, master, first_moment, second_moment, average)


def solution(mesh):
    rows = P("pipe", "dp", "expert", None)
    states = P("pipe", "expert", "dp", None)
    return jax.shard_map(
        shards,
        mesh=mesh,
        in_specs=(rows, rows, rows, P("pipe", "dp", "expert", None, None)) + (states,) * 4,
        out_specs=(states,) * 4,
        check_vma=False,
    )
```

```python
import functools

import jax
import jax.numpy as jnp
from jax import lax
from jax.experimental import pallas as pl
from jax.experimental.pallas import tpu as pltpu
from jax.sharding import PartitionSpec as P

beta_one = 0.9
beta_two = 0.95
epsilon = 1e-08
learn_rate = 0.00022
weight_decay = 0.1
average_decay = 0.999

SIDE = 4
RING = 8
QUARTERS = 4
GROUPS = ((0, 3584),)
SUMS = ("tree", "tree")
TILE = 256
LANES = 128


def torus_pairs(axis):
    pairs = []
    for section in range(4):
        way = 1 if section % 2 == 0 else -1
        for x in range(SIDE):
            for y in range(SIDE):
                to_x, to_y = ((x + way) % SIDE, y) if axis == 0 else (x, (y + way) % SIDE)
                pairs.append((section * 16 + x * SIDE + y, section * 16 + to_x * SIDE + to_y))
    return pairs


def torus_step(value, axis):
    return lax.ppermute(value, ("pipe", "expert"), torus_pairs(axis))


def ring_place(z, kind):
    high, low = z // 4, z % 4
    return (high * 2 + (kind ^ high)) * 4 + low


def ring_step(value, ways):
    pairs = [(ring_place(z, kind), ring_place((z + ways[kind]) % RING, kind)) for kind in range(2) for z in range(RING)]
    return lax.ppermute(value, ("pipe", "dp"), pairs)


def first_kernel(route_ref, gate_ref, cotangent_ref, *out_refs):
    tokens, width = cotangent_ref.shape
    shape = (tokens, LANES)
    lane = lax.broadcasted_iota(jnp.int32, shape, 1)
    expert = lane >> 2
    member = jnp.zeros(shape, jnp.float32)
    weight = jnp.zeros(shape, jnp.float32)
    for k in range(route_ref.shape[1]):
        match = route_ref[:, k : k + 1] == expert
        member = member + jnp.where(match, 1.0, 0.0)
        weight = weight + jnp.where(match, gate_ref[:, k : k + 1], 0.0)
    before = lax.broadcasted_iota(jnp.int32, (tokens, tokens), 1) < lax.broadcasted_iota(jnp.int32, (tokens, tokens), 0)
    position = jnp.dot(
        before.astype(jnp.float32).astype(jnp.bfloat16),
        member.astype(jnp.bfloat16),
        preferred_element_type=jnp.float32,
    )
    high = weight.astype(jnp.bfloat16).astype(jnp.float32)
    middle = (weight - high).astype(jnp.bfloat16).astype(jnp.float32)
    low = weight - high - middle
    kind = lane & 3
    table = jnp.where(member > 0.5, position, -1.0)
    table = jnp.where(kind == 0, table, jnp.where(kind == 1, high, jnp.where(kind == 2, middle, low)))
    table = table.astype(jnp.bfloat16)
    quarter = tokens // QUARTERS
    for q, out_ref in enumerate(out_refs):
        out_ref[:, :width] = cotangent_ref[q * quarter : (q + 1) * quarter, :]
        out_ref[:, width:] = table[q * quarter : (q + 1) * quarter, :]


def first_lines(route, gate, cotangent):
    tokens, width = cotangent.shape
    return pl.pallas_call(
        first_kernel,
        out_shape=[jax.ShapeDtypeStruct((tokens // QUARTERS, width + LANES), jnp.bfloat16)] * QUARTERS,
        compiler_params=pltpu.CompilerParams(vmem_limit_bytes=16 * 1024 * 1024),
        name="first_lines",
    )(route, gate, cotangent)


def rows_kernel(order_ref, *refs):
    hidden_refs, table_refs, out_ref, table_scr = refs[:SIDE], refs[SIDE : SIDE + QUARTERS], refs[-2], refs[-1]
    for q in range(QUARTERS):

        @pl.when(pl.program_id(0) == q)
        def _():
            table_scr[...] = table_refs[q][...].astype(jnp.float32)

    table = table_scr[...]
    lane = lax.broadcasted_iota(jnp.int32, table.shape, 1) - 4 * order_ref[QUARTERS * SIDE]
    slot = jnp.sum(jnp.where(lane == 0, table, 0.0), axis=1, keepdims=True).astype(jnp.int32)
    weight = jnp.sum(jnp.where((lane > 0) & (lane < 4), table, 0.0), axis=1, keepdims=True)
    tokens = table.shape[0] // SIDE
    parts = []
    for s, hidden_ref in enumerate(hidden_refs):
        capacity = hidden_ref.shape[1]
        here = slice(s * tokens, (s + 1) * tokens)
        chosen = lax.broadcasted_iota(jnp.int32, (tokens, capacity), 1) == slot[here]
        picked = jnp.dot(
            chosen.astype(jnp.float32).astype(jnp.bfloat16), hidden_ref[0], preferred_element_type=jnp.float32
        )
        parts.append(picked * weight[here])
    rows = jnp.concatenate(parts, axis=0).T.astype(jnp.bfloat16)
    unit = rows.shape[0] // RING
    for z in range(RING):
        at = (z % 4) * 2 + z // 4
        out_ref[z * unit : (z + 1) * unit, :] = rows[at * unit : (at + 1) * unit, :]


def token_rows(hidden, order, lines):
    sources, capacity, inner = hidden.shape
    height, width = lines[0].shape

    def hidden_spec(s):
        return pl.BlockSpec((1, capacity, inner), lambda i, order_ref, s=s: (order_ref[i * SIDE + s], 0, 0))

    return pl.pallas_call(
        rows_kernel,
        out_shape=jax.ShapeDtypeStruct((inner, QUARTERS * height), jnp.bfloat16),
        grid_spec=pltpu.PrefetchScalarGridSpec(
            num_scalar_prefetch=1,
            grid=(QUARTERS,),
            in_specs=[hidden_spec(s) for s in range(SIDE)]
            + [pl.BlockSpec((height, LANES), lambda i, order_ref: (0, width // LANES - 1))] * QUARTERS,
            out_specs=pl.BlockSpec((inner, height), lambda i, order_ref: (0, i)),
            scratch_shapes=[pltpu.VMEM((height, LANES), jnp.float32)],
        ),
        compiler_params=pltpu.CompilerParams(vmem_limit_bytes=16 * 1024 * 1024),
        cost_estimate=pl.CostEstimate(flops=10**9, bytes_accessed=4 * 10**6, transcendentals=0),
        name="token_rows",
    )(order, *([hidden] * SIDE), *lines)


def assemble_kernel(spans, *refs):
    pieces, outs, sems = refs[: QUARTERS * SIDE], refs[-QUARTERS - 1 : -1], refs[-1]
    tokens = pieces[0].shape[0]
    copies = []
    for q in range(QUARTERS):
        for s in range(SIDE):
            to = 0
            for start, width in spans:
                copies.append(
                    pltpu.make_async_copy(
                        pieces[q * SIDE + s].at[:, start : start + width],
                        outs[q].at[s * tokens : (s + 1) * tokens, to : to + width],
                        sems.at[len(copies)],
                    )
                )
                to += width
    for copy in copies:
        copy.start()
    for copy in copies:
        copy.wait()


def assemble(first, spans, before):
    tokens = first[0][0].shape[0]
    width = sum(w for _, w in spans)
    anywhere = pl.BlockSpec(memory_space=pl.ANY)
    return pl.pallas_call(
        functools.partial(assemble_kernel, spans),
        out_shape=[jax.ShapeDtypeStruct((SIDE * tokens, width), jnp.bfloat16)] * QUARTERS,
        in_specs=[anywhere] * (QUARTERS * SIDE + len(before)),
        out_specs=[anywhere] * QUARTERS,
        scratch_shapes=[pltpu.SemaphoreType.DMA((QUARTERS * SIDE * len(spans),))],
        compiler_params=pltpu.CompilerParams(vmem_limit_bytes=1024 * 1024),
        cost_estimate=pl.CostEstimate(flops=0, bytes_accessed=4 * QUARTERS * SIDE * tokens * width, transcendentals=0),
        name="assemble",
    )(*[piece for pieces in first for piece in pieces], *before)


def contract_kernel(steps, more, *refs):
    rows_refs, pieces, out_ref = refs[:steps], refs[steps : steps * (1 + QUARTERS)], refs[-1]
    total = refs[steps * (1 + QUARTERS)][...] if more else None
    for step, rows_ref in enumerate(rows_refs):
        here = pieces[step * QUARTERS : (step + 1) * QUARTERS]
        cotangent = jnp.concatenate([piece[...] for piece in here], axis=0)
        part = jnp.dot(rows_ref[...], cotangent, preferred_element_type=jnp.float32)
        total = part if total is None else total + part
    out_ref[...] = total.astype(out_ref.dtype)


def contract(rows, lines, width, dtype, more=(), start=0):
    inner, depth = rows[0].shape
    pieces = [piece for step in lines for piece in step]
    height = pieces[0].shape[0]
    return pl.pallas_call(
        functools.partial(contract_kernel, len(rows), len(more)),
        out_shape=jax.ShapeDtypeStruct((inner, width), dtype),
        grid=(width // TILE,),
        in_specs=[pl.BlockSpec((inner, depth), lambda i: (0, 0), pipeline_mode=pl.Buffered(1))] * len(rows)
        + [pl.BlockSpec((height, TILE), lambda i: (0, start // TILE + i))] * len(pieces)
        + [pl.BlockSpec((inner, TILE), lambda i: (0, start // TILE + i))] * len(more),
        out_specs=pl.BlockSpec((inner, TILE), lambda i: (0, i)),
        compiler_params=pltpu.CompilerParams(vmem_limit_bytes=16 * 1024 * 1024),
        cost_estimate=pl.CostEstimate(
            flops=2 * inner * depth * len(rows) * width,
            bytes_accessed=6 * inner * width,
            transcendentals=0,
        ),
        name="contract",
    )(*rows, *pieces, *more)


def ring_sum(terms, height, way):
    def term(owner):
        return lax.dynamic_index_in_dim(terms, owner % RING, 0, keepdims=False).astype(jnp.float32)

    total = term(height - way)
    for step in range(2, RING + 1):
        total = ring_step(total.astype(jnp.bfloat16), (1, -1)).astype(jnp.float32) + term(height - way * step)
    return total


def tree_sum(terms, height):
    def term(distance):
        return lax.dynamic_index_in_dim(terms, (height + distance) % RING, 0, keepdims=False).astype(jnp.float32)

    def send(value, way):
        return ring_step(value.astype(jnp.bfloat16), (way, way)).astype(jnp.float32)

    far = term(RING // 2)
    middle = far.shape[0] // 2
    up, down = send(far[:middle], 1), send(far[middle:], -1)
    near_up, near_down = term(3), term(5)
    up = jnp.concatenate([near_up[:middle] + up, near_up[middle:]], 0)
    down = jnp.concatenate([near_down[:middle], near_down[middle:] + down], 0)
    up, down = send(up, 1), send(down, -1)
    up, down = send(up + term(2), 1), send(down + term(6), -1)
    up, down = send(up + term(1), 1), send(down + term(7), -1)
    return term(0) + up + down


def update(gradient, master, first_moment, second_moment, average):
    moment_one = beta_one * first_moment.astype(jnp.float32) + (1.0 - beta_one) * gradient
    moment_two = beta_two * second_moment.astype(jnp.float32) + (1.0 - beta_two) * gradient * gradient
    master_new = master - learn_rate * (
        moment_one / (jnp.sqrt(moment_two) + epsilon) + weight_decay * master
    )
    average_new = average_decay * average.astype(jnp.float32) + (1.0 - average_decay) * master_new
    return (
        master_new,
        moment_one.astype(jnp.bfloat16),
        moment_two.astype(jnp.bfloat16),
        average_new.astype(jnp.bfloat16),
    )


def shards(cotangent, gates, routes, saved_hidden, master, first_moment, second_moment, average):
    tokens_here = cotangent[0, 0]
    route = routes[0, 0]
    gate = gates[0, 0]
    hidden = saved_hidden[0, 0, 0]
    expert_count = lax.axis_size("expert")
    capacity = hidden.shape[0] // expert_count
    quarter = tokens_here.shape[0] // QUARTERS
    inner = hidden.shape[1]
    me = lax.axis_index("expert")
    section = lax.axis_index("pipe")
    height = (section // 2) * 4 + lax.axis_index("dp")

    first = [[piece] for piece in first_lines(route, gate, tokens_here)]
    for _ in range(SIDE - 1):
        for q in range(QUARTERS):
            first[q].append(torus_step(first[q][-1], 0 if q < 2 else 1))

    way = 1 - 2 * (section % 2)
    steps = jnp.arange(SIDE, dtype=jnp.int32)
    at_x, at_y = me // SIDE, me % SIDE
    along_x = (at_x - way * steps) % SIDE
    along_y = (at_y - way * steps) % SIDE
    order_a = along_x[None, :] * SIDE + along_y[:, None]
    order_b = along_x[:, None] * SIDE + along_y[None, :]
    hidden = hidden.reshape(expert_count, capacity, inner)

    rows, sums, last = [], [], None
    for g, (start, width) in enumerate(GROUPS):
        spans = ((start, width),) if g else ((start, width), (tokens_here.shape[1], LANES))
        lines = [assemble(first, spans, last[2] if g else [])]
        for _ in range(SIDE - 1):
            lines.append([torus_step(lines[-1][q], 1 if q < 2 else 0) for q in range(QUARTERS)])
        if not g:
            for step in range(SIDE):
                order = jnp.concatenate([order_a[step], order_a[step], order_b[step], order_b[step], me[None]])
                rows.append(token_rows(hidden, order, lines[step]))
        part = contract(rows[:-1], lines[:-1], width, jnp.float32)
        half = width // 2
        for at in (0, half):
            sums.append(contract(rows[-1:], lines[-1:], half, jnp.bfloat16, [part], at))
        last = lines

    gradients = []
    for kind, terms in zip(SUMS, sums):
        terms = terms.reshape(RING, -1, terms.shape[1])
        if kind == "ring":
            gradients.append(ring_sum(terms, height, 1 - 2 * (section % 2 ^ section // 2)))
        else:
            gradients.append(tree_sum(terms, height))
    gradient = jnp.concatenate(gradients, 1).reshape(master.shape)
    return update(gradient, master, first_moment, second_moment, average)


def solution(mesh):
    rows = P("pipe", "dp", "expert", None)
    states = P("pipe", "expert", "dp", None)
    return jax.shard_map(
        shards,
        mesh=mesh,
        in_specs=(rows, rows, rows, P("pipe", "dp", "expert", None, None)) + (states,) * 4,
        out_specs=(states,) * 4,
        check_vma=False,
    )
```

```python
import functools

import jax
import jax.numpy as jnp
from jax import lax
from jax.experimental import pallas as pl
from jax.experimental.pallas import tpu as pltpu
from jax.sharding import PartitionSpec as P

beta_one = 0.9
beta_two = 0.95
epsilon = 1e-08
learn_rate = 0.00022
weight_decay = 0.1
average_decay = 0.999

SIDE = 4
RING = 8
QUARTERS = 4
GROUPS = ((0, 3584),)
SUMS = ("tree", "tree")
TILE = 256
LANES = 128


def torus_pairs(axis):
    pairs = []
    for section in range(4):
        way = 1 if section % 2 == 0 else -1
        for x in range(SIDE):
            for y in range(SIDE):
                to_x, to_y = ((x + way) % SIDE, y) if axis == 0 else (x, (y + way) % SIDE)
                pairs.append((section * 16 + x * SIDE + y, section * 16 + to_x * SIDE + to_y))
    return pairs


def torus_step(value, axis):
    return lax.ppermute(value, ("pipe", "expert"), torus_pairs(axis))


def ring_place(z, kind):
    high, low = z // 4, z % 4
    return (high * 2 + (kind ^ high)) * 4 + low


def ring_step(value, ways):
    pairs = [(ring_place(z, kind), ring_place((z + ways[kind]) % RING, kind)) for kind in range(2) for z in range(RING)]
    return lax.ppermute(value, ("pipe", "dp"), pairs)


def first_kernel(route_ref, gate_ref, cotangent_ref, *out_refs):
    tokens, width = cotangent_ref.shape
    shape = (tokens, LANES)
    lane = lax.broadcasted_iota(jnp.int32, shape, 1)
    expert = lane >> 2
    member = jnp.zeros(shape, jnp.float32)
    weight = jnp.zeros(shape, jnp.float32)
    for k in range(route_ref.shape[1]):
        match = route_ref[:, k : k + 1] == expert
        member = member + jnp.where(match, 1.0, 0.0)
        weight = weight + jnp.where(match, gate_ref[:, k : k + 1], 0.0)
    before = lax.broadcasted_iota(jnp.int32, (tokens, tokens), 1) < lax.broadcasted_iota(jnp.int32, (tokens, tokens), 0)
    position = jnp.dot(
        before.astype(jnp.float32).astype(jnp.bfloat16),
        member.astype(jnp.bfloat16),
        preferred_element_type=jnp.float32,
    )
    high = weight.astype(jnp.bfloat16).astype(jnp.float32)
    middle = (weight - high).astype(jnp.bfloat16).astype(jnp.float32)
    low = weight - high - middle
    kind = lane & 3
    table = jnp.where(member > 0.5, position, -1.0)
    table = jnp.where(kind == 0, table, jnp.where(kind == 1, high, jnp.where(kind == 2, middle, low)))
    table = table.astype(jnp.bfloat16)
    quarter = tokens // QUARTERS
    for q, out_ref in enumerate(out_refs):
        out_ref[:, :width] = cotangent_ref[q * quarter : (q + 1) * quarter, :]
        out_ref[:, width:] = table[q * quarter : (q + 1) * quarter, :]


def first_lines(route, gate, cotangent):
    tokens, width = cotangent.shape
    return pl.pallas_call(
        first_kernel,
        out_shape=[jax.ShapeDtypeStruct((tokens // QUARTERS, width + LANES), jnp.bfloat16)] * QUARTERS,
        compiler_params=pltpu.CompilerParams(vmem_limit_bytes=16 * 1024 * 1024),
        name="first_lines",
    )(route, gate, cotangent)


def rows_kernel(order_ref, *refs):
    hidden_refs, table_refs, out_ref, table_scr = refs[:SIDE], refs[SIDE : SIDE + QUARTERS], refs[-2], refs[-1]
    for q in range(QUARTERS):

        @pl.when(pl.program_id(0) == q)
        def _():
            table_scr[...] = table_refs[q][...].astype(jnp.float32)

    table = table_scr[...]
    lane = lax.broadcasted_iota(jnp.int32, table.shape, 1) - 4 * order_ref[QUARTERS * SIDE]
    slot = jnp.sum(jnp.where(lane == 0, table, 0.0), axis=1, keepdims=True).astype(jnp.int32)
    weight = jnp.sum(jnp.where((lane > 0) & (lane < 4), table, 0.0), axis=1, keepdims=True)
    tokens = table.shape[0] // SIDE
    parts = []
    for s, hidden_ref in enumerate(hidden_refs):
        capacity = hidden_ref.shape[1]
        here = slice(s * tokens, (s + 1) * tokens)
        chosen = lax.broadcasted_iota(jnp.int32, (tokens, capacity), 1) == slot[here]
        picked = jnp.dot(
            chosen.astype(jnp.float32).astype(jnp.bfloat16), hidden_ref[0], preferred_element_type=jnp.float32
        )
        parts.append(picked * weight[here])
    rows = jnp.concatenate(parts, axis=0).T.astype(jnp.bfloat16)
    unit = rows.shape[0] // RING
    for z in range(RING):
        at = (z % 4) * 2 + z // 4
        out_ref[z * unit : (z + 1) * unit, :] = rows[at * unit : (at + 1) * unit, :]


def token_rows(hidden, order, lines):
    sources, capacity, inner = hidden.shape
    height, width = lines[0].shape

    def hidden_spec(s):
        return pl.BlockSpec((1, capacity, inner), lambda i, order_ref, s=s: (order_ref[i * SIDE + s], 0, 0))

    return pl.pallas_call(
        rows_kernel,
        out_shape=jax.ShapeDtypeStruct((inner, QUARTERS * height), jnp.bfloat16),
        grid_spec=pltpu.PrefetchScalarGridSpec(
            num_scalar_prefetch=1,
            grid=(QUARTERS,),
            in_specs=[hidden_spec(s) for s in range(SIDE)]
            + [pl.BlockSpec((height, LANES), lambda i, order_ref: (0, width // LANES - 1))] * QUARTERS,
            out_specs=pl.BlockSpec((inner, height), lambda i, order_ref: (0, i)),
            scratch_shapes=[pltpu.VMEM((height, LANES), jnp.float32)],
        ),
        compiler_params=pltpu.CompilerParams(vmem_limit_bytes=16 * 1024 * 1024),
        cost_estimate=pl.CostEstimate(flops=10**9, bytes_accessed=4 * 10**6, transcendentals=0),
        name="token_rows",
    )(order, *([hidden] * SIDE), *lines)


def assemble_kernel(spans, *refs):
    pieces, outs, sems = refs[: QUARTERS * SIDE], refs[-QUARTERS - 1 : -1], refs[-1]
    tokens = pieces[0].shape[0]
    copies = []
    for q in range(QUARTERS):
        for s in range(SIDE):
            to = 0
            for start, width in spans:
                copies.append(
                    pltpu.make_async_copy(
                        pieces[q * SIDE + s].at[:, start : start + width],
                        outs[q].at[s * tokens : (s + 1) * tokens, to : to + width],
                        sems.at[len(copies)],
                    )
                )
                to += width
    for copy in copies:
        copy.start()
    for copy in copies:
        copy.wait()


def assemble(first, spans, before):
    tokens = first[0][0].shape[0]
    width = sum(w for _, w in spans)
    anywhere = pl.BlockSpec(memory_space=pl.ANY)
    return pl.pallas_call(
        functools.partial(assemble_kernel, spans),
        out_shape=[jax.ShapeDtypeStruct((SIDE * tokens, width), jnp.bfloat16)] * QUARTERS,
        in_specs=[anywhere] * (QUARTERS * SIDE + len(before)),
        out_specs=[anywhere] * QUARTERS,
        scratch_shapes=[pltpu.SemaphoreType.DMA((QUARTERS * SIDE * len(spans),))],
        compiler_params=pltpu.CompilerParams(vmem_limit_bytes=1024 * 1024),
        cost_estimate=pl.CostEstimate(flops=0, bytes_accessed=4 * QUARTERS * SIDE * tokens * width, transcendentals=0),
        name="assemble",
    )(*[piece for pieces in first for piece in pieces], *before)


def contract_kernel(steps, more, *refs):
    rows_refs, pieces, out_ref = refs[:steps], refs[steps : steps * (1 + QUARTERS)], refs[-1]
    total = refs[steps * (1 + QUARTERS)][...].astype(jnp.float32) if more else None
    for step, rows_ref in enumerate(rows_refs):
        here = pieces[step * QUARTERS : (step + 1) * QUARTERS]
        cotangent = jnp.concatenate([piece[...] for piece in here], axis=0)
        part = jnp.dot(rows_ref[...], cotangent, preferred_element_type=jnp.float32)
        total = part if total is None else total + part
    out_ref[...] = total.astype(out_ref.dtype)


def contract(rows, lines, width, dtype, more=(), start=0):
    inner, depth = rows[0].shape
    pieces = [piece for step in lines for piece in step]
    height = pieces[0].shape[0]
    return pl.pallas_call(
        functools.partial(contract_kernel, len(rows), len(more)),
        out_shape=jax.ShapeDtypeStruct((inner, width), dtype),
        grid=(width // TILE,),
        in_specs=[pl.BlockSpec((inner, depth), lambda i: (0, 0), pipeline_mode=pl.Buffered(1))] * len(rows)
        + [pl.BlockSpec((height, TILE), lambda i: (0, start // TILE + i))] * len(pieces)
        + [pl.BlockSpec((inner, TILE), lambda i: (0, start // TILE + i))] * len(more),
        out_specs=pl.BlockSpec((inner, TILE), lambda i: (0, i)),
        compiler_params=pltpu.CompilerParams(vmem_limit_bytes=16 * 1024 * 1024),
        cost_estimate=pl.CostEstimate(
            flops=2 * inner * depth * len(rows) * width,
            bytes_accessed=6 * inner * width,
            transcendentals=0,
        ),
        name="contract",
    )(*rows, *pieces, *more)


def ring_sum(terms, height, way):
    def term(owner):
        return lax.dynamic_index_in_dim(terms, owner % RING, 0, keepdims=False).astype(jnp.float32)

    total = term(height - way)
    for step in range(2, RING + 1):
        total = ring_step(total.astype(jnp.bfloat16), (1, -1)).astype(jnp.float32) + term(height - way * step)
    return total


def tree_sum(terms, height):
    def term(distance):
        return lax.dynamic_index_in_dim(terms, (height + distance) % RING, 0, keepdims=False).astype(jnp.float32)

    def send(value, way):
        return ring_step(value.astype(jnp.bfloat16), (way, way)).astype(jnp.float32)

    far = term(RING // 2)
    middle = far.shape[0] // 2
    up, down = send(far[:middle], 1), send(far[middle:], -1)
    near_up, near_down = term(3), term(5)
    up = jnp.concatenate([near_up[:middle] + up, near_up[middle:]], 0)
    down = jnp.concatenate([near_down[:middle], near_down[middle:] + down], 0)
    up, down = send(up, 1), send(down, -1)
    up, down = send(up + term(2), 1), send(down + term(6), -1)
    up, down = send(up + term(1), 1), send(down + term(7), -1)
    return term(0) + up + down


def update(gradient, master, first_moment, second_moment, average):
    moment_one = beta_one * first_moment.astype(jnp.float32) + (1.0 - beta_one) * gradient
    moment_two = beta_two * second_moment.astype(jnp.float32) + (1.0 - beta_two) * gradient * gradient
    master_new = master - learn_rate * (
        moment_one / (jnp.sqrt(moment_two) + epsilon) + weight_decay * master
    )
    average_new = average_decay * average.astype(jnp.float32) + (1.0 - average_decay) * master_new
    return (
        master_new,
        moment_one.astype(jnp.bfloat16),
        moment_two.astype(jnp.bfloat16),
        average_new.astype(jnp.bfloat16),
    )


def shards(cotangent, gates, routes, saved_hidden, master, first_moment, second_moment, average):
    tokens_here = cotangent[0, 0]
    route = routes[0, 0]
    gate = gates[0, 0]
    hidden = saved_hidden[0, 0, 0]
    expert_count = lax.axis_size("expert")
    capacity = hidden.shape[0] // expert_count
    quarter = tokens_here.shape[0] // QUARTERS
    inner = hidden.shape[1]
    me = lax.axis_index("expert")
    section = lax.axis_index("pipe")
    height = (section // 2) * 4 + lax.axis_index("dp")

    first = [[piece] for piece in first_lines(route, gate, tokens_here)]
    for _ in range(SIDE - 1):
        for q in range(QUARTERS):
            first[q].append(torus_step(first[q][-1], 0 if q < 2 else 1))

    way = 1 - 2 * (section % 2)
    steps = jnp.arange(SIDE, dtype=jnp.int32)
    at_x, at_y = me // SIDE, me % SIDE
    along_x = (at_x - way * steps) % SIDE
    along_y = (at_y - way * steps) % SIDE
    order_a = along_x[None, :] * SIDE + along_y[:, None]
    order_b = along_x[:, None] * SIDE + along_y[None, :]
    hidden = hidden.reshape(expert_count, capacity, inner)

    rows, sums, last = [], [], None
    for g, (start, width) in enumerate(GROUPS):
        spans = ((start, width),) if g else ((start, width), (tokens_here.shape[1], LANES))
        lines = [assemble(first, spans, last[2] if g else [])]
        for _ in range(SIDE - 1):
            lines.append([torus_step(lines[-1][q], 1 if q < 2 else 0) for q in range(QUARTERS)])
        if not g:
            for step in range(SIDE):
                order = jnp.concatenate([order_a[step], order_a[step], order_b[step], order_b[step], me[None]])
                rows.append(token_rows(hidden, order, lines[step]))
        part = contract(rows[:-1], lines[:-1], width, jnp.bfloat16)
        half = width // 2
        for at in (0, half):
            sums.append(contract(rows[-1:], lines[-1:], half, jnp.bfloat16, [part], at))
        last = lines

    gradients = []
    for kind, terms in zip(SUMS, sums):
        terms = terms.reshape(RING, -1, terms.shape[1])
        if kind == "ring":
            gradients.append(ring_sum(terms, height, 1 - 2 * (section % 2 ^ section // 2)))
        else:
            gradients.append(tree_sum(terms, height))
    gradient = jnp.concatenate(gradients, 1).reshape(master.shape)
    return update(gradient, master, first_moment, second_moment, average)


def solution(mesh):
    rows = P("pipe", "dp", "expert", None)
    states = P("pipe", "expert", "dp", None)
    return jax.shard_map(
        shards,
        mesh=mesh,
        in_specs=(rows, rows, rows, P("pipe", "dp", "expert", None, None)) + (states,) * 4,
        out_specs=(states,) * 4,
        check_vma=False,
    )
```
